512 devices in a mesh: dp: 16 (over x_hi, y), expert: 32 (over x_lo, z, core).
Axes of the slice: x: 4 (x_hi: 2, x_lo: 2; x = x_hi * 2 + x_lo), y: 8, z: 8, core: 2. Of those that a mesh axis runs over, the one named last changes fastest.
Arguments:
- projection_gradient: bfloat16 [2, 1536, 2, 12288], P(None, 'dp', None, 'expert'), may hold values from -6 to 6
- acts: bfloat16 [5120, 12288], P('dp', 'expert'), may hold values from -6 to 6
- routes: int32 [12288, 2], P('expert'), may hold values from 0 to 31, all different within a row; in each aligned block of 384 rows (0 to 383, 384 to 767, ...) at most 30 rows name the same one
- gates: bfloat16 [12288, 2], P('expert'), may hold values from 0.049804688 to 1
- tenants: int32 [12288], P('expert'), may hold values from 0 to 7
- levels: bfloat16 [32, 2, 5120, 1536], P('expert', None, 'dp'), may hold values from -8 to 7, as said below
- scales: bfloat16 [32, 2, 80, 1536], P('expert', None, 'dp'), may hold values from 0.0029907227 to 0.010986328
- adapter_first_factors: bfloat16 [32, 2, 5120, 128], P('expert', None, 'dp'), may hold values from -0.1875 to 0.1875
- adapter_second_factors: bfloat16 [32, 2, 1536, 128], P('expert', None, 'dp'), may hold values from -0.15625 to 0.15625
Outputs:
- input_grad: bfloat16 [5120, 12288], P('dp', 'expert')
- first_factor_gradient: float32 [32, 2, 5120, 128], P('expert', None, 'dp')
- second_factor_gradient: float32 [32, 2, 1536, 128], P('expert', None, 'dp')
The draws below stay inside these ranges and needn't reach their ends.
Inputs may be any that keep to these rules, and one draw needn't show every extreme that they name: `routes`: each token names 2 different experts. Among the tokens of one index of expert (an aligned block of 384 tokens) at most 30 name any one expert, a bound that some block reaches. `levels`: whole numbers held as bfloat16.
All inputs are finite; a program needn't handle non-finite values.
Results may differ from the reference program's by a relative error of at most 0.007.
Values may be sent and summed in bfloat16 or wider, within the bound.
No kernel may reach another device: no remote copies, remote signals or barrier semaphores. Data moves between devices by JAX's collectives and lax.ppermute only.
A program may use at most 128 MiB of HBM per device.

```python
import math
import jax
import jax.numpy as jnp
import numpy as np
from jax import lax

MODEL_WIDTH = 5120
HIDDEN_UNITS = 1536
ADAPTER_RANK = 16
TENANT_COUNT = 8
GROUP = 64
TOPK = 2
TOK_DEV = 384
EXPERT_COUNT = 32
TOKENS = 12288
CAP = 30
N_EXPERT = 32


def draw_levels(key, part):
    key = jax.random.fold_in(key, 11)
    drawn = jax.random.randint(key, (EXPERT_COUNT, 2, MODEL_WIDTH, HIDDEN_UNITS), -8, 8)
    return drawn.astype(jnp.bfloat16)


def touch_ends(result, rng, least, top_value):
    shape = result.shape
    place = [jax.random.randint(jax.random.fold_in(rng, axis), (), 0, shape[axis]) for axis in range(len(shape))]
    result = result.at[tuple(place)].set(least)
    longest = shape.index(max(shape))
    place[longest] = (place[longest] + 1) % shape[longest]
    return result.at[tuple(place)].set(top_value)


def level_of(key, extent, split, least, high):
    loudness = 1.0
    for dim, parts in split:
        draws = jax.random.uniform(jax.random.fold_in(jax.random.fold_in(key, 6), dim), (parts,), jnp.float32, least / len(split), high / len(split))
        loudness = loudness * jnp.repeat(jnp.exp(draws), extent[dim] // parts).reshape((-1,) + (1,) * (len(extent) - 1 - dim))
    return loudness


def routed_block(rng, own, number, rows, count, top, bound, skew):
    ranking = jax.random.permutation(rng, count)
    crowded, usual = portions_of(count, rows * top, bound, skew, True), portions_of(count, rows * top, bound, skew, False)
    places = jnp.arange(count)

    def named(lengths, turn):
        used = int((lengths > 0).sum())
        fixed = max(1, used // 4)
        moved = fixed + (places - fixed + turn * (used - fixed)) % max(1, count - fixed)
        return jnp.zeros((count,), jnp.int32).at[ranking[jnp.where(places < fixed, places, moved)]].set(jnp.asarray(lengths, jnp.int32))

    lengths = jnp.where(number % 4 == 0, named(crowded, number // 4), named(usual, number - number // 4 - 1))
    mixed = jax.random.permutation(jax.random.fold_in(own, 3), count)
    donor, receiver = mixed[0:count // 2 * 2:2], mixed[1:count // 2 * 2:2]
    slack = jnp.minimum(lengths[donor] - 1, bound - lengths[receiver]) // 2
    slack = jnp.where((donor == ranking[0]) | (receiver == ranking[0]) | (lengths[receiver] == 0), 0, jnp.maximum(slack, 0))
    moved = jax.random.randint(jax.random.fold_in(own, 4), (count // 2,), 0, 1 << 20) % (slack + 1)
    lengths = lengths.at[donor].add(-moved).at[receiver].add(moved)
    members = jnp.searchsorted(jnp.cumsum(lengths), jnp.arange(rows * top), side="right").astype(jnp.int32)
    table = members.reshape(top, rows).T
    table = table[jax.random.permutation(jax.random.fold_in(own, 1), rows)]
    turn = jax.random.randint(jax.random.fold_in(own, 2), (rows, 1), 0, top)
    return jnp.take_along_axis(table, (jnp.arange(top)[None, :] + turn) % top, axis=1)


def portions_of(number_of, total, bound, slope, full):
    portions = [(1 << 20) // math.isqrt(rank ** slope) + 1 for rank in range(1, number_of + 1)]
    largest = bound if full else min(bound, max(-(-total // number_of), total * portions[0] // sum(portions)))
    least = 1 if total - largest >= number_of - 1 else 0
    holding, rest = [largest] + [least] * (number_of - 1), total - largest - least * (number_of - 1)
    while rest > 0:
        free = [i for i in range(1, number_of) if holding[i] < largest] or [i for i in range(1, number_of) if holding[i] < bound]
        pool, remaining = sum([portions[i] for i in free]), rest
        for i in free:
            more = min(bound - holding[i], max(1, remaining * portions[i] // pool), rest)
            holding[i] = holding[i] + more
            rest = rest - more
    return np.array(holding)


def bell_draw(stream_key, extent, deviation, bound, cuts=(), held_as=jnp.bfloat16):
    result = jax.random.normal(stream_key, extent, jnp.float32) * deviation
    if len(cuts) > 0:
        result = level_of(stream_key, extent, cuts, -0.22, 0.18) * result
    return jnp.clip(result, min=-bound, max=bound).astype(held_as)


def setup_inputs(seed: int = 0) -> dict:
    arg_keys = jax.random.split(jax.random.key(seed), 10)
    projection_gradient = bell_draw(arg_keys[0], (2, HIDDEN_UNITS, TOPK, TOKENS), 1.0, 6.0, ((1, 16), (3, 32)))
    acts = bell_draw(arg_keys[1], (MODEL_WIDTH, TOKENS), 1.0, 6.0, ((0, 16), (1, 32)))
    routes_keys = jax.random.split(jax.random.fold_in(arg_keys[2], 1), TOKENS // TOK_DEV)
    routes_turns = jax.random.permutation(jax.random.fold_in(arg_keys[2], 3), TOKENS // TOK_DEV)
    routes = jax.vmap(lambda own, number: routed_block(jax.random.fold_in(arg_keys[2], 2), own, number, TOK_DEV, EXPERT_COUNT, TOPK, CAP, 2))(routes_keys, routes_turns).reshape((TOKENS, TOPK))
    gates = jnp.clip(jnp.exp(math.log(1.0) - 2.9996462 * jax.random.uniform(arg_keys[3], (TOKENS, TOPK), jnp.float32) ** level_of(arg_keys[3], (TOKENS, TOPK), ((0, 32),), -0.2, 0.2)), 0.049804688, 1.0).astype(jnp.bfloat16)
    tenants = touch_ends(jax.random.randint(arg_keys[4], (TOKENS,), 0, TENANT_COUNT), jax.random.fold_in(arg_keys[4], 1), 0, TENANT_COUNT - 1).astype(jnp.int32)
    levels = draw_levels(jax.random.fold_in(arg_keys[9], 71), 0)
    scales = jnp.clip(jnp.exp(math.log(0.010986328) - 1.30113655 * jax.random.uniform(arg_keys[6], (EXPERT_COUNT, 2, MODEL_WIDTH // GROUP, HIDDEN_UNITS), jnp.float32) ** level_of(arg_keys[6], (EXPERT_COUNT, 2, MODEL_WIDTH // GROUP, HIDDEN_UNITS), ((0, 32), (2, 16)), -0.2, 0.2)), 0.0029907227, 0.010986328).astype(jnp.bfloat16)
    adapter_first_factors = bell_draw(arg_keys[7], (EXPERT_COUNT, 2, MODEL_WIDTH, TENANT_COUNT * ADAPTER_RANK), 1024 ** -0.5, 0.1875, ((0, 32), (2, 16)))
    adapter_second_factors = bell_draw(arg_keys[8], (EXPERT_COUNT, 2, HIDDEN_UNITS, TENANT_COUNT * ADAPTER_RANK), HIDDEN_UNITS ** -0.5, 0.15625, ((0, 32), (2, 16)))
    return {"projection_gradient": projection_gradient, "acts": acts, "routes": routes, "gates": gates, "tenants": tenants, "levels": levels, "scales": scales, "adapter_first_factors": adapter_first_factors, "adapter_second_factors": adapter_second_factors}


ADAPTER_SCALE = 2.0


def dequantize(level_block, scale_block):
    planes, rows, width = level_block.shape
    grouped = level_block.astype(jnp.float32).reshape(planes, rows // GROUP, GROUP, width)
    return (grouped * scale_block.astype(jnp.float32)[:, :, None, :]).reshape(planes, rows, width).astype(jnp.bfloat16)


def tenant_select(values, onehot):
    planes, count, columns = values.shape
    shaped = values.reshape(planes, count, TENANT_COUNT, columns // TENANT_COUNT)
    return jnp.sum(shaped * onehot[None, :, :, None], axis=2)


def tenant_expand(values, onehot):
    planes, count, rank_cols = values.shape
    return (values[:, :, None, :] * onehot[None, :, :, None]).reshape(planes, count, TENANT_COUNT * rank_cols)


def reference(projection_gradient, acts, routes, gates, tenants, levels, scales, adapter_first_factors, adapter_second_factors):
    pairs = TOPK * TOKENS
    slots = N_EXPERT * CAP
    expert_of = routes.T.reshape(-1).astype(jnp.int32)
    gate_flat = gates.T.reshape(-1).astype(jnp.float32)
    grad_flat = projection_gradient.reshape(2, HIDDEN_UNITS, pairs)
    token_of = jnp.arange(pairs, dtype=jnp.int32) % TOKENS
    positions = jnp.arange(slots, dtype=jnp.int32)
    tenant_ids = jnp.arange(TENANT_COUNT, dtype=jnp.int32)
    zero_half = jnp.zeros((), jnp.bfloat16)
    zero_full = jnp.zeros((), jnp.float32)

    def expert_update(total_sum, inputs):
        index, level_block, scale_block, adapter_first, adapter_second = inputs
        match = expert_of == index
        count = jnp.sum(match.astype(jnp.int32))
        chosen = jnp.nonzero(match, size=slots, fill_value=0)[0].astype(jnp.int32)
        valid = positions < count
        token = token_of[chosen]
        gate_values = jnp.where(valid, gate_flat[chosen], zero_full)
        grads = jnp.where(valid[None, None, :], grad_flat[:, :, chosen], zero_half)
        inputs_x = jnp.where(valid[None, :], acts[:, token], zero_half)
        onehot_ten = (tenants[token].astype(jnp.int32)[:, None] == tenant_ids[None, :]).astype(jnp.float32)
        weights = dequantize(level_block, scale_block)
        frozen = jnp.dot(weights[0], grads[0], preferred_element_type=jnp.float32) + jnp.dot(weights[1], grads[1], preferred_element_type=jnp.float32)
        down_sum = tenant_select(jnp.einsum("dp,jdc->jpc", inputs_x.astype(jnp.float32), adapter_first.astype(jnp.float32)), onehot_ten)
        back_sum = tenant_select(jnp.einsum("jhp,jhc->jpc", grads.astype(jnp.float32), adapter_second.astype(jnp.float32)), onehot_ten)
        scale_factor = ADAPTER_SCALE * gate_values[None, :, None]
        down_scaled = tenant_expand(down_sum * scale_factor, onehot_ten).astype(jnp.bfloat16)
        back_scaled = tenant_expand(back_sum * scale_factor, onehot_ten).astype(jnp.bfloat16)
        adapter_dx = jnp.einsum("jdc,jpc->dp", adapter_first.astype(jnp.float32), back_scaled.astype(jnp.float32))
        pair_dx = (gate_values[None, :] * frozen + adapter_dx).astype(jnp.bfloat16)
        first_factor_gradient = jnp.einsum("dp,jpc->jdc", inputs_x.astype(jnp.float32), back_scaled.astype(jnp.float32))
        second_factor_gradient = jnp.einsum("jhp,jpc->jhc", grads.astype(jnp.float32), down_scaled.astype(jnp.float32))
        update = jnp.where(valid[None, :], pair_dx.astype(jnp.float32), zero_full)
        total_sum = total_sum.at[:, token].add(update)
        return total_sum, (first_factor_gradient, second_factor_gradient)

    start_column = jnp.zeros((MODEL_WIDTH, TOKENS), jnp.float32)
    total_sum, (first_factor_gradient, second_factor_gradient) = lax.scan(expert_update, start_column, (jnp.arange(EXPERT_COUNT, dtype=jnp.int32), levels, scales, adapter_first_factors, adapter_second_factors))
    return total_sum.astype(jnp.bfloat16), first_factor_gradient, second_factor_gradient
```

```python
import functools

import jax
import jax.numpy as jnp
from jax import lax
from jax.experimental import pallas as pl
from jax.experimental.pallas import tpu as pltpu
from jax.sharding import Mesh
from jax.sharding import PartitionSpec as P

TENANT_COUNT = 8
GROUP = 64
ADAPTER_SCALE = 2.0
BF = jnp.bfloat16
F32 = jnp.float32


def dot(a, b, dims):
    return lax.dot_general(a, b, (dims, ((), ())), preferred_element_type=F32)


def dequantize(level_block, scale_block):
    planes, rows, width = level_block.shape
    grouped = level_block.astype(F32).reshape(planes, rows // GROUP, GROUP, width)
    return (
        (grouped * scale_block.astype(F32)[:, :, None, :]).reshape(planes, rows, width).astype(BF)
    )


def pair_kernel(
    hid, rank, z_ref, second_ref, gate_ref, row_ref, weight_ref, first_ref, dx_ref, back_ref, wide_ref
):
    depth, cols = second_ref.shape

    @pl.when(pl.program_id(0) == 0)
    def _():
        row = lax.broadcasted_iota(jnp.int32, (depth, cols), 0)
        plane = (row // hid) % 2
        second = second_ref[...].astype(F32)
        wide_ref[:, :cols] = jnp.where(plane == 0, second, 0.0).astype(BF)
        wide_ref[:, cols:] = jnp.where(plane == 1, second, 0.0).astype(BF)

    z = z_ref[...]
    tile = z.shape[1]
    gate = gate_ref[:, 0:1].astype(F32)
    tenant = gate_ref[:, 1:2].astype(F32)
    lane = lax.broadcasted_iota(jnp.int32, (tile, 2 * cols), 1)
    mine = ((lane % cols) // rank).astype(F32) == tenant
    back = dot(z, wide_ref[...], ((0,), (0,)))
    back_scaled = jnp.where(mine, back * (ADAPTER_SCALE * gate), 0.0).astype(BF)
    frozen = dot(z, weight_ref[...], ((0,), (0,)))
    out = gate * frozen + dot(back_scaled, first_ref[...], ((1,), (0,)))
    half = out.shape[1] // 2
    dx_ref[0] = out[:, :half].astype(BF)
    dx_ref[1] = out[:, half:].astype(BF)
    across = dot(wide_ref[...], z, ((0,), (0,)))
    tenant_row = row_ref[1:2, :].astype(F32)
    for plane in range(2):
        total = jnp.zeros((rank, tile), F32)
        for t in range(cols // rank):
            start = plane * cols + t * rank
            total += jnp.where(tenant_row == float(t), across[start : start + rank], 0.0)
        back_ref[plane * rank : (plane + 1) * rank, :] = total


def pair_call(gathered, slot_rows, slot_cols, weights, first, hid, rank, slots):
    depth, wide = gathered.shape
    cols = wide - slots
    width = weights.shape[1]
    tile = 256 if slots % 256 == 0 else slots
    return pl.pallas_call(
        functools.partial(pair_kernel, hid, rank),
        grid=(slots // tile,),
        in_specs=[
            pl.BlockSpec((depth, tile), lambda i: (0, i)),
            pl.BlockSpec((depth, cols), lambda i: (0, slots // cols)),
            pl.BlockSpec((tile, slot_rows.shape[1]), lambda i: (i, 0)),
            pl.BlockSpec((slot_cols.shape[0], tile), lambda i: (0, i)),
            pl.BlockSpec((depth, width), lambda i: (0, 0)),
            pl.BlockSpec((2 * cols, width), lambda i: (0, 0)),
        ],
        out_specs=[
            pl.BlockSpec((2, tile, width // 2), lambda i: (0, i, 0)),
            pl.BlockSpec((2 * rank, tile), lambda i: (0, i)),
        ],
        out_shape=[
            jax.ShapeDtypeStruct((2, slots, width // 2), BF),
            jax.ShapeDtypeStruct((2 * rank, slots), F32),
        ],
        scratch_shapes=[pltpu.VMEM((depth, 2 * cols), BF)],
        compiler_params=pltpu.CompilerParams(vmem_limit_bytes=40 * 1024 * 1024),
        cost_estimate=pl.CostEstimate(
            flops=2 * slots * depth * (width + 4 * cols),
            bytes_accessed=2 * depth * (wide + width) + 2 * slots * width,
            transcendentals=0,
        ),
    )(gathered, gathered, slot_rows, slot_cols, weights, first)


def on_device(
    projection_gradient,
    acts,
    routes,
    gates,
    tenants,
    levels,
    scales,
    adapter_first_factors,
    adapter_second_factors,
):
    experts = lax.axis_size("expert")
    ring = lax.axis_size("y")
    half = lax.axis_index("xh")
    planes, hid, topk, toks = projection_gradient.shape
    width_rows = acts.shape[0]
    rank = adapter_first_factors.shape[3] // TENANT_COUNT
    cols = TENANT_COUNT * rank
    capacity = 5 * toks * topk // (4 * experts)
    room = -(-capacity // 16) * 16
    slots = experts * room
    own = planes * hid

    expert_ids = lax.broadcasted_iota(jnp.int32, (experts, toks), 0)
    named = [routes[:, k][None, :] == expert_ids for k in range(topk)]
    member = functools.reduce(jnp.logical_or, named).astype(BF)
    before = (
        lax.broadcasted_iota(jnp.int32, (toks, toks), 0)
        < lax.broadcasted_iota(jnp.int32, (toks, toks), 1)
    ).astype(BF)
    place = dot(member, before, ((1,), (0,))).astype(jnp.int32) + expert_ids * room
    position = [jnp.sum(jnp.where(m, place, 0), axis=0) for m in named]
    slot_ids = lax.broadcasted_iota(jnp.int32, (slots, toks), 0)
    chosen = [slot_ids == p[None, :] for p in position]
    select = jnp.concatenate([c.astype(BF) for c in chosen], axis=1)
    select_tok = functools.reduce(jnp.logical_or, chosen).astype(BF)

    spare = -(-(own + 2) // 128) * 128 - own - 2
    sent = jnp.concatenate(
        [
            projection_gradient.reshape(own, topk * toks),
            gates.T.reshape(1, topk * toks),
            jnp.tile(tenants.astype(BF)[None, :], (1, topk)),
            jnp.zeros((spare, topk * toks), BF),
        ],
        axis=0,
    )
    send_z = dot(select, sent, ((1,), (1,))).astype(BF).reshape(experts, room, -1)
    got_z = lax.all_to_all(send_z, "expert", 0, 0, tiled=True).reshape(slots, -1)
    across_z = got_z.T
    own_z = across_z[:own]
    slot_rows = got_z[:, own : own + 2]
    slot_cols = across_z[own : own + 2]

    adapter_first = adapter_first_factors[0]
    adapter_second = adapter_second_factors[0].reshape(own, cols)
    payload = jnp.concatenate([own_z, adapter_second], axis=1)
    gathered = lax.all_gather(payload, "y", axis=0, tiled=True)

    weights = dequantize(levels[0], scales[0])
    mid = weights.shape[2] // 2
    low, high = weights[:, :, :mid], weights[:, :, mid:]
    swap = [(0, 1), (1, 0)]
    got_w = lax.ppermute(jnp.where(half == 0, high, low), "xh", swap)
    kept_w = jnp.where(half == 0, low, high)
    got_first = lax.ppermute(adapter_first, "xh", swap)

    def both(kept, got):
        return jnp.stack([jnp.where(half == 0, kept, got), jnp.where(half == 0, got, kept)])

    pair_w = both(kept_w, got_w)
    pair_w = (
        pair_w.reshape(2, planes, width_rows, ring, hid)
        .transpose(3, 1, 4, 0, 2)
        .reshape(ring * own, 2 * width_rows)
    )
    pair_first = both(adapter_first, got_first).transpose(1, 3, 0, 2)
    pair_first = pair_first.reshape(planes * cols, 2 * width_rows)

    send_x = dot(select_tok, acts, ((1,), (1,))).astype(BF).reshape(experts, room, width_rows)
    got_x = lax.all_to_all(send_x, "expert", 0, 0, tiled=True).reshape(slots, width_rows)
    tenant_row = slot_cols[1].astype(F32)
    one = tenant_row[None, :] == jnp.arange(TENANT_COUNT, dtype=F32)[:, None]
    down = lax.dot_general(
        adapter_first, got_x, (((1,), (1,)), ((), ())), preferred_element_type=F32
    ).reshape(planes, TENANT_COUNT, rank, slots)
    down = jnp.sum(jnp.where(one[None, :, None, :], down, 0.0), axis=1).reshape(
        planes * rank, slots
    )
    step = 1
    while step < ring:
        down = down + lax.ppermute(down, "y", [(i, i ^ step) for i in range(ring)])
        step *= 2

    pair_dx, back = pair_call(
        gathered, slot_rows, slot_cols, pair_w, pair_first, hid, rank, slots
    )
    returned = lax.all_to_all(
        pair_dx.reshape(2 * experts, room, width_rows), ("xh", "expert"), 0, 0, tiled=True
    ).reshape(2, slots, width_rows)
    input_grad = dot(returned[0], select_tok, ((0,), (0,))) + dot(
        returned[1], select_tok, ((0,), (0,))
    )

    ranks = jnp.concatenate([down, back], axis=0)
    ranks = ranks + lax.ppermute(ranks, "xh", swap)
    scaled = (ranks * (ADAPTER_SCALE * slot_cols[0].astype(F32))[None, :]).astype(BF)
    spread = jnp.where(
        one[None, :, None, :], scaled.reshape(2 * planes, 1, rank, slots), jnp.zeros((), BF)
    ).reshape(2, planes, cols, slots)
    second_grad = jnp.stack(
        [
            dot(own_z[j * hid : (j + 1) * hid], spread[0, j], ((1,), (1,)))
            for j in range(planes)
        ]
    )
    first_grad = jnp.stack([dot(got_x, spread[1, j].T, ((0,), (0,))) for j in range(planes)])
    return input_grad.astype(BF), first_grad[None], second_grad[None]


def solution(mesh):
    groups, experts = mesh.devices.shape
    split = Mesh(mesh.devices.reshape(2, groups // 2, experts), ("xh", "y", "expert"))
    dp = ("xh", "y")
    factors = P("expert", None, dp, None)
    return jax.shard_map(
        on_device,
        mesh=split,
        in_specs=(
            P(None, dp, None, "expert"),
            P(dp, "expert"),
            P("expert", None),
            P("expert", None),
            P("expert"),
            factors,
            factors,
            factors,
            factors,
        ),
        out_specs=(P(dp, "expert"), factors, factors),
        check_vma=False,
    )
```

```python
import functools

import jax
import jax.numpy as jnp
from jax import lax
from jax.experimental import pallas as pl
from jax.experimental.pallas import tpu as pltpu
from jax.sharding import Mesh
from jax.sharding import PartitionSpec as P

TENANT_COUNT = 8
GROUP = 64
ADAPTER_SCALE = 2.0
BF = jnp.bfloat16
F32 = jnp.float32


def dot(a, b, dims):
    return lax.dot_general(a, b, (dims, ((), ())), preferred_element_type=F32)


def weight_kernel(group, half_ref, level_ref, scale_ref, first_ref, kept_ref, sent_ref):
    planes, rows, width = level_ref.shape
    mid = width // 2
    near = pl.multiple_of(half_ref[0] * mid, 128)
    far = pl.multiple_of((1 - half_ref[0]) * mid, 128)

    def rounded(j, start):
        parts = []
        for g in range(rows // group):
            level = level_ref[j, g * group : (g + 1) * group, pl.ds(start, mid)].astype(F32)
            scale = scale_ref[j, g : g + 1, pl.ds(start, mid)].astype(F32)
            parts.append((level * scale).astype(BF))
        return jnp.concatenate(parts, axis=0)

    for j in range(planes):
        sent_ref[j, :, :mid] = rounded(j, far)
        sent_ref[j, :, mid:] = first_ref[j]
        kept_ref[j] = rounded(j, near).T


def weight_call(half, levels, scales, first):
    planes, rows, width = levels.shape
    mid, cols = width // 2, first.shape[2]
    vmem = pl.BlockSpec(memory_space=pltpu.VMEM)
    return pl.pallas_call(
        functools.partial(weight_kernel, GROUP),
        in_specs=[pl.BlockSpec(memory_space=pltpu.SMEM), vmem, vmem, vmem],
        out_specs=[vmem, vmem],
        out_shape=[
            jax.ShapeDtypeStruct((planes, mid, rows), BF),
            jax.ShapeDtypeStruct((planes, rows, mid + cols), BF),
        ],
        compiler_params=pltpu.CompilerParams(vmem_limit_bytes=16 * 1024 * 1024),
        cost_estimate=pl.CostEstimate(
            flops=planes * rows * width, bytes_accessed=4 * planes * rows * width, transcendentals=0
        ),
    )(half, levels, scales, first)


def pair_kernel(
    rank, tile, own, half_ref, z_ref, rows_ref, cols_ref, kept_ref, got_ref, first_ref,
    dx_ref, back_ref, turned_ref
):
    ring, planes, hid, wide = z_ref.shape
    room, depth, width = dx_ref.shape[2] * 128 // kept_ref.shape[2], kept_ref.shape[1], kept_ref.shape[2]
    slots = dx_ref.shape[1] * room
    tiles, cols = slots // tile, wide - slots
    some, full = tile // room, width // 128
    for j in range(planes):
        turned_ref[j] = got_ref[j, :, :depth].T
    at = own
    half = half_ref[0]
    lane = lax.broadcasted_iota(jnp.int32, (tile, cols), 1)

    def step(i, carry):
        place = pl.ds(pl.multiple_of(i * tile, tile), tile)
        gate = rows_ref[place, at : at + 1].astype(F32)
        tenant = rows_ref[place, at + 1 : at + 2].astype(F32)
        tenant_row = cols_ref[own + 1 : own + 2, place].astype(F32)
        mine = (lane // rank).astype(F32) == tenant
        z, scaled = [], []
        for j in range(planes):
            z.append(z_ref[:, j, :, place].reshape(ring * hid, tile))
            second = z_ref[:, j, :, slots:].reshape(ring * hid, cols)
            back = dot(z[j], second, ((0,), (0,)))
            scaled.append(jnp.where(mine, back * (ADAPTER_SCALE * gate), 0.0).astype(BF))
            across = dot(second, z[j], ((0,), (0,)))
            total = jnp.zeros((rank, tile), F32)
            for t in range(cols // rank):
                part = across[t * rank : (t + 1) * rank]
                total += jnp.where(tenant_row == float(t), part, 0.0)
            back_ref[j * rank : (j + 1) * rank, place] = total
        firsts = [first_ref[j] for j in range(planes)], [got_ref[j, :, depth:] for j in range(planes)]
        both = ((half, kept_ref, firsts[0]), (1 - half, turned_ref, firsts[1]))
        from_experts = pl.ds(i * some, some)
        for where, weight, first in both:
            frozen = sum(dot(z[j], weight[j], ((0,), (0,))) for j in range(planes))
            extra = sum(dot(scaled[j], first[j], ((1,), (1,))) for j in range(planes))
            dx = (gate * frozen + extra).astype(BF).reshape(some, room, width)
            for c in range(full):
                dx_ref[where, from_experts, c * room : (c + 1) * room, :] = dx[:, :, c * 128 : (c + 1) * 128]
            rest = dx[:, :, full * 128 :]
            rest = jnp.concatenate([rest[:, : room // 2], rest[:, room // 2 :]], axis=2)
            dx_ref[where, from_experts, full * room :, :] = rest
        return carry

    lax.fori_loop(0, tiles, step, 0)


def pair_call(half, gathered, got_z, across_z, kept, got, first, rank, own, slots, experts):
    ring, planes, hid, wide = gathered.shape
    cols = wide - slots
    depth, width = kept.shape[1:]
    tile = 256 if slots % 256 == 0 else slots
    vmem = pl.BlockSpec(memory_space=pltpu.VMEM)
    return pl.pallas_call(
        functools.partial(pair_kernel, rank, tile, own),
        in_specs=[
            pl.BlockSpec(memory_space=pltpu.SMEM),
            vmem,
            vmem,
            vmem,
            vmem,
            vmem,
            vmem,
        ],
        out_specs=[vmem, vmem],
        out_shape=[
            jax.ShapeDtypeStruct((2, experts, slots // experts * width // 128, 128), BF),
            jax.ShapeDtypeStruct((planes * rank, slots), F32),
        ],
        scratch_shapes=[pltpu.VMEM((planes, depth, width), BF)],
        compiler_params=pltpu.CompilerParams(vmem_limit_bytes=24 * 1024 * 1024),
        cost_estimate=pl.CostEstimate(
            flops=2 * slots * planes * depth * (2 * width + 2 * cols),
            bytes_accessed=2 * planes * depth * (wide + 2 * width) + 4 * slots * width,
            transcendentals=0,
        ),
    )(half, gathered, got_z, across_z, kept, got, first)


def combine_kernel(got_ref, select_ref, out_ref):
    halves, experts, _, lanes = got_ref.shape
    room, toks = select_ref.shape[1:]
    full = out_ref.shape[0] // lanes

    def total(start, size, chosen):
        parts = [got_ref[h, :, start : start + size, :] for h in range(halves)]
        parts = [p.reshape(experts * size, lanes) for p in parts]
        return sum(dot(p, chosen, ((0,), (0,))) for p in parts)

    select = select_ref[...].reshape(experts * room, toks)
    for c in range(full):
        out_ref[c * lanes : (c + 1) * lanes, :] = total(c * room, room, select).astype(BF)
    low = select_ref[:, : room // 2].reshape(experts * room // 2, toks)
    high = select_ref[:, room // 2 :].reshape(experts * room // 2, toks)
    first = total(full * room, room // 2, low)[: lanes // 2]
    second = total(full * room, room // 2, high)[lanes // 2 :]
    out_ref[full * lanes :, :] = (first + second).astype(BF)


def combine_call(got, select, width):
    vmem = pl.BlockSpec(memory_space=pltpu.VMEM)
    return pl.pallas_call(
        combine_kernel,
        in_specs=[vmem, vmem],
        out_specs=vmem,
        out_shape=jax.ShapeDtypeStruct((width, select.shape[2]), BF),
        compiler_params=pltpu.CompilerParams(vmem_limit_bytes=16 * 1024 * 1024),
        cost_estimate=pl.CostEstimate(
            flops=2 * got.size * select.shape[2], bytes_accessed=4 * got.size, transcendentals=0
        ),
    )(got, select)


def on_device(
    projection_gradient,
    acts,
    routes,
    gates,
    tenants,
    levels,
    scales,
    adapter_first_factors,
    adapter_second_factors,
):
    experts = lax.axis_size("expert")
    ring = lax.axis_size("y")
    half = lax.axis_index("xh")
    planes, hid, topk, toks = projection_gradient.shape
    width_rows = acts.shape[0]
    rank = adapter_first_factors.shape[3] // TENANT_COUNT
    cols = TENANT_COUNT * rank
    capacity = 5 * toks * topk // (4 * experts)
    room = -(-capacity // 16) * 16
    slots = experts * room
    own = planes * hid

    expert_ids = lax.broadcasted_iota(jnp.int32, (experts, toks), 0)
    named = [routes[:, k][None, :] == expert_ids for k in range(topk)]
    member = functools.reduce(jnp.logical_or, named).astype(BF)
    before = (
        lax.broadcasted_iota(jnp.int32, (toks, toks), 0)
        < lax.broadcasted_iota(jnp.int32, (toks, toks), 1)
    ).astype(BF)
    place = dot(member, before, ((1,), (0,))).astype(jnp.int32) + expert_ids * room
    position = [jnp.sum(jnp.where(m, place, 0), axis=0) for m in named]
    slot_ids = lax.broadcasted_iota(jnp.int32, (slots, toks), 0)
    chosen = [slot_ids == p[None, :] for p in position]
    select = jnp.concatenate([c.astype(BF) for c in chosen], axis=1)
    select_tok = functools.reduce(jnp.logical_or, chosen).astype(BF)

    side = 64
    sent = jnp.concatenate(
        [
            projection_gradient.reshape(own, topk * toks),
            gates.T.reshape(1, topk * toks),
            jnp.tile(tenants.astype(BF)[None, :], (1, topk)),
            jnp.zeros((side - 2, topk * toks), BF),
        ],
        axis=0,
    )
    send_z = dot(select, sent, ((1,), (1,))).astype(BF).reshape(experts, room, -1)
    send_z, levels, scales, acts = lax.optimization_barrier((send_z, levels, scales, acts))
    got_z = lax.all_to_all(send_z, "expert", 0, 0, tiled=True).reshape(slots, -1)

    adapter_first = adapter_first_factors[0]
    adapter_second = adapter_second_factors[0].reshape(own, cols)
    swap = [(0, 1), (1, 0)]
    kept_w, send_w = weight_call(half.reshape(1), levels[0], scales[0], adapter_first)
    send_x = dot(select_tok, acts, ((1,), (1,))).astype(BF).reshape(experts, room, width_rows)
    got_w = lax.ppermute(send_w, "xh", swap)
    got_z, send_x, kept_w = lax.optimization_barrier((got_z, send_x, kept_w))

    across_z = got_z.T
    own_z = across_z[:own]
    payload = jnp.concatenate([own_z, adapter_second], axis=1)
    gathered = lax.all_gather(payload.reshape(planes, hid, slots + cols), "y", axis=0, tiled=False)

    got_x = lax.all_to_all(send_x, "expert", 0, 0, tiled=True).reshape(slots, width_rows)
    gate_row = across_z[own].astype(F32)
    tenant_row = across_z[own + 1].astype(F32)
    one = tenant_row[None, :] == jnp.arange(TENANT_COUNT, dtype=F32)[:, None]
    down = lax.dot_general(
        adapter_first, got_x, (((1,), (1,)), ((), ())), preferred_element_type=F32
    ).reshape(planes, TENANT_COUNT, rank, slots)
    down = jnp.sum(jnp.where(one[None, :, None, :], down, 0.0), axis=1).reshape(
        planes * rank, slots
    )
    exchanges = [[(i, i ^ (1 << k)) for i in range(ring)] for k in range(ring.bit_length() - 1)]
    down = down + lax.ppermute(down, "y", exchanges[0])
    down, got_w = lax.optimization_barrier((down, got_w))
    down = down + lax.ppermute(down, "y", exchanges[1])
    down, got_w = lax.optimization_barrier((down, got_w))

    pair_dx, back = pair_call(
        half.reshape(1), gathered, got_z, across_z, kept_w, got_w, adapter_first,
        rank, own, slots, experts
    )
    returned = lax.all_to_all(
        pair_dx.reshape((2 * experts,) + pair_dx.shape[2:]), ("xh", "expert"), 0, 0, tiled=True
    ).reshape(pair_dx.shape)
    for pairs in exchanges[2:]:
        down = down + lax.ppermute(down, "y", pairs)
    ranks = jnp.concatenate([down, back], axis=0)
    ranks = ranks + lax.ppermute(ranks, "xh", swap)
    scaled = (ranks * (ADAPTER_SCALE * gate_row)[None, :]).astype(BF)
    spread = jnp.where(
        one[None, :, None, :], scaled.reshape(2 * planes, 1, rank, slots), jnp.zeros((), BF)
    ).reshape(2, planes, cols, slots)
    second_grad = jnp.stack(
        [
            dot(own_z[j * hid : (j + 1) * hid], spread[0, j], ((1,), (1,)))
            for j in range(planes)
        ]
    )
    first_grad = jnp.stack([dot(got_x, spread[1, j].T, ((0,), (0,))) for j in range(planes)])
    returned, first_grad, second_grad = lax.optimization_barrier((returned, first_grad, second_grad))
    input_grad = combine_call(returned, select_tok.reshape(experts, room, toks), width_rows)
    return input_grad, first_grad[None], second_grad[None]


def solution(mesh):
    groups, experts = mesh.devices.shape
    split = Mesh(mesh.devices.reshape(2, groups // 2, experts), ("xh", "y", "expert"))
    dp = ("xh", "y")
    factors = P("expert", None, dp, None)
    return jax.shard_map(
        on_device,
        mesh=split,
        in_specs=(
            P(None, dp, None, "expert"),
            P(dp, "expert"),
            P("expert", None),
            P("expert", None),
            P("expert"),
            factors,
            factors,
            factors,
            factors,
        ),
        out_specs=(P(dp, "expert"), factors, factors),
        check_vma=False,
    )
```

```python
import functools

import jax
import jax.numpy as jnp
from jax import lax
from jax.experimental import pallas as pl
from jax.experimental.pallas import tpu as pltpu
from jax.sharding import Mesh
from jax.sharding import PartitionSpec as P

TENANT_COUNT = 8
GROUP = 64
ADAPTER_SCALE = 2.0
BF = jnp.bfloat16
F32 = jnp.float32


def dot(a, b, dims):
    return lax.dot_general(a, b, (dims, ((), ())), preferred_element_type=F32)


def route_kernel(room, side, route_ref, gate_ref, tenant_ref, grad_ref, send_ref, select_ref, full_ref):
    topk, toks = route_ref.shape
    own, slots = grad_ref.shape[0], send_ref.shape[0]
    expert_ids = lax.broadcasted_iota(jnp.int32, (slots // room, toks), 0)
    named = [route_ref[k : k + 1, :] == expert_ids for k in range(topk)]
    member = sum(jnp.where(m, 1.0, 0.0) for m in named).astype(BF)
    row = lax.broadcasted_iota(jnp.int32, (toks, toks), 0)
    before = jnp.where(row < lax.broadcasted_iota(jnp.int32, (toks, toks), 1), 1.0, 0.0).astype(BF)
    place = dot(member, before, ((1,), (0,))).astype(jnp.int32) + expert_ids * room
    slot_ids = lax.broadcasted_iota(jnp.int32, (slots, toks), 0)
    line = lax.broadcasted_iota(jnp.int32, (side, toks), 0)
    tenant = tenant_ref[...].astype(F32)
    total, either = 0.0, 0.0
    for k in range(topk):
        position = jnp.sum(jnp.where(named[k], place, 0), axis=0, keepdims=True)
        chosen = jnp.where(slot_ids == position, 1.0, 0.0)
        either = either + chosen
        gate = gate_ref[k : k + 1, :].astype(F32)
        extra = jnp.where(line == 0, gate, jnp.where(line == 1, tenant, 0.0))
        full_ref[:own, :] = grad_ref[:, k * toks : (k + 1) * toks]
        full_ref[own:, :] = extra.astype(BF)
        total = total + dot(chosen.astype(BF), full_ref[...], ((1,), (1,)))
    send_ref[...] = total.astype(BF)
    select_ref[...] = either.astype(BF)


def route_call(routes, gates, tenants, grads, experts, room, side):
    toks, own, slots = tenants.shape[1], grads.shape[0], experts * room
    vmem = pl.BlockSpec(memory_space=pltpu.VMEM)
    return pl.pallas_call(
        functools.partial(route_kernel, room, side),
        in_specs=[vmem] * 4,
        out_specs=[vmem, vmem],
        out_shape=[
            jax.ShapeDtypeStruct((slots, own + side), BF),
            jax.ShapeDtypeStruct((slots, toks), BF),
        ],
        scratch_shapes=[pltpu.VMEM((own + side, toks), BF)],
        compiler_params=pltpu.CompilerParams(vmem_limit_bytes=16 * 1024 * 1024),
        cost_estimate=pl.CostEstimate(
            flops=4 * slots * toks * (own + side), bytes_accessed=4 * slots * toks, transcendentals=0
        ),
    )(routes, gates, tenants, grads)


def weight_kernel(group, half_ref, level_ref, scale_ref, first_ref, kept_ref, sent_ref):
    planes, rows, width = level_ref.shape
    mid = width // 2
    near = pl.multiple_of(half_ref[0] * mid, 128)
    far = pl.multiple_of((1 - half_ref[0]) * mid, 128)

    def rounded(j, start):
        parts = []
        for g in range(rows // group):
            level = level_ref[j, g * group : (g + 1) * group, pl.ds(start, mid)].astype(F32)
            scale = scale_ref[j, g : g + 1, pl.ds(start, mid)].astype(F32)
            parts.append((level * scale).astype(BF))
        return jnp.concatenate(parts, axis=0)

    for j in range(planes):
        sent_ref[j, :, :mid] = rounded(j, far)
        sent_ref[j, :, mid:] = first_ref[j]
        kept_ref[j] = rounded(j, near).T


def weight_call(half, levels, scales, first):
    planes, rows, width = levels.shape
    mid, cols = width // 2, first.shape[2]
    vmem = pl.BlockSpec(memory_space=pltpu.VMEM)
    return pl.pallas_call(
        functools.partial(weight_kernel, GROUP),
        in_specs=[pl.BlockSpec(memory_space=pltpu.SMEM), vmem, vmem, vmem],
        out_specs=[vmem, vmem],
        out_shape=[
            jax.ShapeDtypeStruct((planes, mid, rows), BF),
            jax.ShapeDtypeStruct((planes, rows, mid + cols), BF),
        ],
        compiler_params=pltpu.CompilerParams(vmem_limit_bytes=16 * 1024 * 1024),
        cost_estimate=pl.CostEstimate(
            flops=planes * rows * width, bytes_accessed=4 * planes * rows * width, transcendentals=0
        ),
    )(half, levels, scales, first)


def pair_kernel(
    rank, tile, own, half_ref, z_ref, rows_ref, cols_ref, kept_ref, got_ref, first_ref,
    dx_ref, back_ref, turned_ref
):
    ring, planes, hid, wide = z_ref.shape
    room, depth, width = dx_ref.shape[2] * 128 // kept_ref.shape[2], kept_ref.shape[1], kept_ref.shape[2]
    slots = dx_ref.shape[1] * room
    tiles, cols = slots // tile, wide - slots
    some, full = tile // room, width // 128
    for j in range(planes):
        turned_ref[j] = got_ref[j, :, :depth].T
    at = own
    half = half_ref[0]
    lane = lax.broadcasted_iota(jnp.int32, (tile, cols), 1)

    def step(i, carry):
        place = pl.ds(pl.multiple_of(i * tile, tile), tile)
        gate = rows_ref[place, at : at + 1].astype(F32)
        tenant = rows_ref[place, at + 1 : at + 2].astype(F32)
        tenant_row = cols_ref[own + 1 : own + 2, place].astype(F32)
        mine = (lane // rank).astype(F32) == tenant
        z, scaled = [], []
        for j in range(planes):
            z.append(z_ref[:, j, :, place].reshape(ring * hid, tile).T)
            second = z_ref[:, j, :, slots:].reshape(ring * hid, cols)
            back = dot(z[j], second, ((1,), (0,)))
            scaled.append(jnp.where(mine, back * (ADAPTER_SCALE * gate), 0.0).astype(BF))
            across = back.T
            total = jnp.zeros((rank, tile), F32)
            for t in range(cols // rank):
                part = across[t * rank : (t + 1) * rank]
                total += jnp.where(tenant_row == float(t), part, 0.0)
            back_ref[j * rank : (j + 1) * rank, place] = total
        firsts = [first_ref[j] for j in range(planes)], [got_ref[j, :, depth:] for j in range(planes)]
        both = ((half, kept_ref, firsts[0]), (1 - half, turned_ref, firsts[1]))
        from_experts = pl.ds(i * some, some)
        for where, weight, first in both:
            frozen = sum(dot(z[j], weight[j], ((1,), (0,))) for j in range(planes))
            extra = sum(dot(scaled[j], first[j], ((1,), (1,))) for j in range(planes))
            dx = (gate * frozen + extra).astype(BF).reshape(some, room, width)
            for c in range(full):
                dx_ref[where, from_experts, c * room : (c + 1) * room, :] = dx[:, :, c * 128 : (c + 1) * 128]
            rest = dx[:, :, full * 128 :]
            rest = jnp.concatenate([rest[:, : room // 2], rest[:, room // 2 :]], axis=2)
            dx_ref[where, from_experts, full * room :, :] = rest
        return carry

    lax.fori_loop(0, tiles, step, 0)


def pair_call(half, gathered, got_z, across_z, kept, got, first, rank, own, slots, experts):
    ring, planes, hid, wide = gathered.shape
    cols = wide - slots
    depth, width = kept.shape[1:]
    tile = 256 if slots % 256 == 0 else slots
    vmem = pl.BlockSpec(memory_space=pltpu.VMEM)
    return pl.pallas_call(
        functools.partial(pair_kernel, rank, tile, own),
        in_specs=[
            pl.BlockSpec(memory_space=pltpu.SMEM),
            vmem,
            vmem,
            vmem,
            vmem,
            vmem,
            vmem,
        ],
        out_specs=[vmem, vmem],
        out_shape=[
            jax.ShapeDtypeStruct((2, experts, slots // experts * width // 128, 128), BF),
            jax.ShapeDtypeStruct((planes * rank, slots), F32),
        ],
        scratch_shapes=[pltpu.VMEM((planes, depth, width), BF)],
        compiler_params=pltpu.CompilerParams(vmem_limit_bytes=24 * 1024 * 1024),
        cost_estimate=pl.CostEstimate(
            flops=2 * slots * planes * depth * (2 * width + 2 * cols),
            bytes_accessed=2 * planes * depth * (wide + 2 * width) + 4 * slots * width,
            transcendentals=0,
        ),
    )(half, gathered, got_z, across_z, kept, got, first)


def combine_kernel(got_ref, select_ref, out_ref):
    halves, experts, _, lanes = got_ref.shape
    room, toks = select_ref.shape[1:]
    full = out_ref.shape[0] // lanes

    def total(start, size, chosen):
        parts = [got_ref[h, :, start : start + size, :] for h in range(halves)]
        parts = [p.reshape(experts * size, lanes) for p in parts]
        return sum(dot(p, chosen, ((0,), (0,))) for p in parts)

    select = select_ref[...].reshape(experts * room, toks)
    for c in range(full):
        out_ref[c * lanes : (c + 1) * lanes, :] = total(c * room, room, select).astype(BF)
    low = select_ref[:, : room // 2].reshape(experts * room // 2, toks)
    high = select_ref[:, room // 2 :].reshape(experts * room // 2, toks)
    first = total(full * room, room // 2, low)[: lanes // 2]
    second = total(full * room, room // 2, high)[lanes // 2 :]
    out_ref[full * lanes :, :] = (first + second).astype(BF)


def combine_call(got, select, width):
    vmem = pl.BlockSpec(memory_space=pltpu.VMEM)
    return pl.pallas_call(
        combine_kernel,
        in_specs=[vmem, vmem],
        out_specs=vmem,
        out_shape=jax.ShapeDtypeStruct((width, select.shape[2]), BF),
        compiler_params=pltpu.CompilerParams(vmem_limit_bytes=16 * 1024 * 1024),
        cost_estimate=pl.CostEstimate(
            flops=2 * got.size * select.shape[2], bytes_accessed=4 * got.size, transcendentals=0
        ),
    )(got, select)


def on_device(
    projection_gradient,
    acts,
    routes,
    gates,
    tenants,
    levels,
    scales,
    adapter_first_factors,
    adapter_second_factors,
):
    experts = lax.axis_size("expert")
    ring = lax.axis_size("y")
    half = lax.axis_index("xh")
    planes, hid, topk, toks = projection_gradient.shape
    width_rows = acts.shape[0]
    rank = adapter_first_factors.shape[3] // TENANT_COUNT
    cols = TENANT_COUNT * rank
    capacity = 5 * toks * topk // (4 * experts)
    room = -(-capacity // 16) * 16
    slots = experts * room
    own = planes * hid

    side = 64
    send_z, select_tok = route_call(
        routes.T,
        gates.T,
        tenants.reshape(1, toks),
        projection_gradient.reshape(own, topk * toks),
        experts, room, side
    )
    send_z = send_z.reshape(experts, room, own + side)
    send_z, levels, scales, acts = lax.optimization_barrier((send_z, levels, scales, acts))
    got_z = lax.all_to_all(send_z, "expert", 0, 0, tiled=True).reshape(slots, -1)

    adapter_first = adapter_first_factors[0]
    adapter_second = adapter_second_factors[0].reshape(own, cols)
    swap = [(0, 1), (1, 0)]
    kept_w, send_w = weight_call(half.reshape(1), levels[0], scales[0], adapter_first)
    send_x = dot(select_tok, acts, ((1,), (1,))).astype(BF).reshape(experts, room, width_rows)
    got_w = lax.ppermute(send_w, "xh", swap)
    got_z, send_x, kept_w = lax.optimization_barrier((got_z, send_x, kept_w))

    across_z = got_z.T
    own_z = across_z[:own]
    payload = jnp.concatenate([own_z, adapter_second], axis=1)
    gathered = lax.all_gather(payload.reshape(planes, hid, slots + cols), "y", axis=0, tiled=False)

    got_x = lax.all_to_all(send_x, "expert", 0, 0, tiled=True).reshape(slots, width_rows)
    gate_row = across_z[own].astype(F32)
    tenant_row = across_z[own + 1].astype(F32)
    one = tenant_row[None, :] == jnp.arange(TENANT_COUNT, dtype=F32)[:, None]
    down = lax.dot_general(
        adapter_first, got_x, (((1,), (1,)), ((), ())), preferred_element_type=F32
    ).reshape(planes, TENANT_COUNT, rank, slots)
    down = jnp.sum(jnp.where(one[None, :, None, :], down, 0.0), axis=1).reshape(
        planes * rank, slots
    )
    down = down + lax.ppermute(down, "xh", swap)
    down, got_w = lax.optimization_barrier((down, got_w))
    downs = lax.all_gather(down, "y", axis=0, tiled=False)

    pair_dx, back = pair_call(
        half.reshape(1), gathered, got_z, across_z, kept_w, got_w, adapter_first,
        rank, own, slots, experts
    )
    returned = lax.all_to_all(
        pair_dx.reshape((2 * experts,) + pair_dx.shape[2:]), ("xh", "expert"), 0, 0, tiled=True
    ).reshape(pair_dx.shape)
    ranks = jnp.concatenate(
        [jnp.sum(downs, axis=0), back + lax.ppermute(back, "xh", swap)], axis=0
    )
    scaled = (ranks * (ADAPTER_SCALE * gate_row)[None, :]).astype(BF)
    spread = jnp.where(
        one[None, :, None, :], scaled.reshape(2 * planes, 1, rank, slots), jnp.zeros((), BF)
    ).reshape(2, planes, cols, slots)
    second_grad = jnp.stack(
        [
            dot(own_z[j * hid : (j + 1) * hid], spread[0, j], ((1,), (1,)))
            for j in range(planes)
        ]
    )
    first_grad = jnp.stack([dot(got_x, spread[1, j].T, ((0,), (0,))) for j in range(planes)])
    returned, first_grad, second_grad = lax.optimization_barrier((returned, first_grad, second_grad))
    input_grad = combine_call(returned, select_tok.reshape(experts, room, toks), width_rows)
    return input_grad, first_grad[None], second_grad[None]


def solution(mesh):
    groups, experts = mesh.devices.shape
    split = Mesh(mesh.devices.reshape(2, groups // 2, experts), ("xh", "y", "expert"))
    dp = ("xh", "y")
    factors = P("expert", None, dp, None)
    return jax.shard_map(
        on_device,
        mesh=split,
        in_specs=(
            P(None, dp, None, "expert"),
            P(dp, "expert"),
            P("expert", None),
            P("expert", None),
            P("expert"),
            factors,
            factors,
            factors,
            factors,
        ),
        out_specs=(P(dp, "expert"), factors, factors),
        check_vma=False,
    )
```

```python
import functools

import jax
import jax.numpy as jnp
from jax import lax
from jax.experimental import pallas as pl
from jax.experimental.pallas import tpu as pltpu
from jax.sharding import Mesh
from jax.sharding import PartitionSpec as P

TENANT_COUNT = 8
GROUP = 64
ADAPTER_SCALE = 2.0
BF = jnp.bfloat16
F32 = jnp.float32


def dot(a, b, dims):
    return lax.dot_general(a, b, (dims, ((), ())), preferred_element_type=F32)


def route_kernel(room, side, route_ref, gate_ref, tenant_ref, grad_ref, send_ref, select_ref, full_ref):
    topk, toks = route_ref.shape
    own, slots = grad_ref.shape[0], send_ref.shape[0]
    expert_ids = lax.broadcasted_iota(jnp.int32, (slots // room, toks), 0)
    named = [route_ref[k : k + 1, :] == expert_ids for k in range(topk)]
    member = sum(jnp.where(m, 1.0, 0.0) for m in named).astype(BF)
    row = lax.broadcasted_iota(jnp.int32, (toks, toks), 0)
    before = jnp.where(row < lax.broadcasted_iota(jnp.int32, (toks, toks), 1), 1.0, 0.0).astype(BF)
    place = dot(member, before, ((1,), (0,))).astype(jnp.int32) + expert_ids * room
    slot_ids = lax.broadcasted_iota(jnp.int32, (slots, toks), 0)
    line = lax.broadcasted_iota(jnp.int32, (side, toks), 0)
    tenant = tenant_ref[...].astype(F32)
    total, either = 0.0, 0.0
    for k in range(topk):
        position = jnp.sum(jnp.where(named[k], place, 0), axis=0, keepdims=True)
        chosen = jnp.where(slot_ids == position, 1.0, 0.0)
        either = either + chosen
        gate = gate_ref[k : k + 1, :].astype(F32)
        extra = jnp.where(line == 0, gate, jnp.where(line == 1, tenant, 0.0))
        full_ref[:own, :] = grad_ref[:, k * toks : (k + 1) * toks]
        full_ref[own:, :] = extra.astype(BF)
        total = total + dot(chosen.astype(BF), full_ref[...], ((1,), (1,)))
    send_ref[...] = total.astype(BF)
    select_ref[...] = either.astype(BF)


def route_call(routes, gates, tenants, grads, experts, room, side):
    toks, own, slots = tenants.shape[1], grads.shape[0], experts * room
    vmem = pl.BlockSpec(memory_space=pltpu.VMEM)
    return pl.pallas_call(
        functools.partial(route_kernel, room, side),
        in_specs=[vmem] * 4,
        out_specs=[vmem, vmem],
        out_shape=[
            jax.ShapeDtypeStruct((slots, own + side), BF),
            jax.ShapeDtypeStruct((slots, toks), BF),
        ],
        scratch_shapes=[pltpu.VMEM((own + side, toks), BF)],
        compiler_params=pltpu.CompilerParams(vmem_limit_bytes=16 * 1024 * 1024),
        cost_estimate=pl.CostEstimate(
            flops=4 * slots * toks * (own + side), bytes_accessed=4 * slots * toks, transcendentals=0
        ),
    )(routes, gates, tenants, grads)


def weight_kernel(group, half_ref, level_ref, scale_ref, first_ref, kept_ref, sent_ref):
    planes, rows, width = level_ref.shape
    mid = width // 2
    near = pl.multiple_of(half_ref[0] * mid, 128)
    far = pl.multiple_of((1 - half_ref[0]) * mid, 128)

    def rounded(j, start):
        parts = []
        for g in range(rows // group):
            level = level_ref[j, g * group : (g + 1) * group, pl.ds(start, mid)].astype(F32)
            scale = scale_ref[j, g : g + 1, pl.ds(start, mid)].astype(F32)
            parts.append((level * scale).astype(BF))
        return jnp.concatenate(parts, axis=0)

    for j in range(planes):
        sent_ref[j, :, :mid] = rounded(j, far)
        sent_ref[j, :, mid:] = first_ref[j]
        kept_ref[j] = rounded(j, near).T


def weight_call(half, levels, scales, first):
    planes, rows, width = levels.shape
    mid, cols = width // 2, first.shape[2]
    vmem = pl.BlockSpec(memory_space=pltpu.VMEM)
    return pl.pallas_call(
        functools.partial(weight_kernel, GROUP),
        in_specs=[pl.BlockSpec(memory_space=pltpu.SMEM), vmem, vmem, vmem],
        out_specs=[vmem, vmem],
        out_shape=[
            jax.ShapeDtypeStruct((planes, mid, rows), BF),
            jax.ShapeDtypeStruct((planes, rows, mid + cols), BF),
        ],
        compiler_params=pltpu.CompilerParams(vmem_limit_bytes=16 * 1024 * 1024),
        cost_estimate=pl.CostEstimate(
            flops=planes * rows * width, bytes_accessed=4 * planes * rows * width, transcendentals=0
        ),
    )(half, levels, scales, first)


def pair_kernel(
    rank, tile, own, half_ref, z_ref, rows_ref, cols_ref, kept_ref, got_ref, first_ref,
    dx_ref, back_ref, turned_ref
):
    ring, planes, hid, wide = z_ref.shape
    room, depth, width = dx_ref.shape[2] * 128 // kept_ref.shape[2], kept_ref.shape[1], kept_ref.shape[2]
    slots = dx_ref.shape[1] * room
    tiles, cols = slots // tile, wide - slots
    some, full = tile // room, width // 128
    for j in range(planes):
        turned_ref[j] = got_ref[j, :, :depth].T
    at = own
    half = half_ref[0]
    lane = lax.broadcasted_iota(jnp.int32, (tile, cols), 1)

    def step(i):
        place = pl.ds(i * tile, tile)
        gate = rows_ref[place, at : at + 1].astype(F32)
        tenant = rows_ref[place, at + 1 : at + 2].astype(F32)
        tenant_row = cols_ref[own + 1 : own + 2, place].astype(F32)
        mine = (lane // rank).astype(F32) == tenant
        z, scaled = [], []
        for j in range(planes):
            z.append(z_ref[:, j, :, place].reshape(ring * hid, tile).T)
            second = z_ref[:, j, :, slots:].reshape(ring * hid, cols)
            back = dot(z[j], second, ((1,), (0,)))
            scaled.append(jnp.where(mine, back * (ADAPTER_SCALE * gate), 0.0).astype(BF))
            across = back.T
            total = jnp.zeros((rank, tile), F32)
            for t in range(cols // rank):
                part = across[t * rank : (t + 1) * rank]
                total += jnp.where(tenant_row == float(t), part, 0.0)
            back_ref[j * rank : (j + 1) * rank, place] = total
        firsts = [first_ref[j] for j in range(planes)], [got_ref[j, :, depth:] for j in range(planes)]
        both = ((half, kept_ref, firsts[0]), (1 - half, turned_ref, firsts[1]))
        from_experts = pl.ds(i * some, some)
        for where, weight, first in both:
            frozen = sum(dot(z[j], weight[j], ((1,), (0,))) for j in range(planes))
            extra = sum(dot(scaled[j], first[j], ((1,), (1,))) for j in range(planes))
            dx = (gate * frozen + extra).astype(BF).reshape(some, room, width)
            for c in range(full):
                dx_ref[where, from_experts, c * room : (c + 1) * room, :] = dx[:, :, c * 128 : (c + 1) * 128]
            rest = dx[:, :, full * 128 :]
            rest = jnp.concatenate([rest[:, : room // 2], rest[:, room // 2 :]], axis=2)
            dx_ref[where, from_experts, full * room :, :] = rest

    for i in range(tiles):
        step(i)


def pair_call(half, gathered, got_z, across_z, kept, got, first, rank, own, slots, experts):
    ring, planes, hid, wide = gathered.shape
    cols = wide - slots
    depth, width = kept.shape[1:]
    tile = 256 if slots % 256 == 0 else slots
    vmem = pl.BlockSpec(memory_space=pltpu.VMEM)
    return pl.pallas_call(
        functools.partial(pair_kernel, rank, tile, own),
        in_specs=[
            pl.BlockSpec(memory_space=pltpu.SMEM),
            vmem,
            vmem,
            vmem,
            vmem,
            vmem,
            vmem,
        ],
        out_specs=[vmem, vmem],
        out_shape=[
            jax.ShapeDtypeStruct((2, experts, slots // experts * width // 128, 128), BF),
            jax.ShapeDtypeStruct((planes * rank, slots), F32),
        ],
        scratch_shapes=[pltpu.VMEM((planes, depth, width), BF)],
        compiler_params=pltpu.CompilerParams(vmem_limit_bytes=48 * 1024 * 1024),
        cost_estimate=pl.CostEstimate(
            flops=2 * slots * planes * depth * (2 * width + 2 * cols),
            bytes_accessed=2 * planes * depth * (wide + 2 * width) + 4 * slots * width,
            transcendentals=0,
        ),
    )(half, gathered, got_z, across_z, kept, got, first)


def combine_kernel(got_ref, select_ref, out_ref):
    halves, experts, _, lanes = got_ref.shape
    room, toks = select_ref.shape[1:]
    full = out_ref.shape[0] // lanes

    def total(start, size, chosen):
        parts = [got_ref[h, :, start : start + size, :] for h in range(halves)]
        parts = [p.reshape(experts * size, lanes) for p in parts]
        return sum(dot(p, chosen, ((0,), (0,))) for p in parts)

    select = select_ref[...].reshape(experts * room, toks)
    for c in range(full):
        out_ref[c * lanes : (c + 1) * lanes, :] = total(c * room, room, select).astype(BF)
    low = select_ref[:, : room // 2].reshape(experts * room // 2, toks)
    high = select_ref[:, room // 2 :].reshape(experts * room // 2, toks)
    first = total(full * room, room // 2, low)[: lanes // 2]
    second = total(full * room, room // 2, high)[lanes // 2 :]
    out_ref[full * lanes :, :] = (first + second).astype(BF)


def combine_call(got, select, width):
    vmem = pl.BlockSpec(memory_space=pltpu.VMEM)
    return pl.pallas_call(
        combine_kernel,
        in_specs=[vmem, vmem],
        out_specs=vmem,
        out_shape=jax.ShapeDtypeStruct((width, select.shape[2]), BF),
        compiler_params=pltpu.CompilerParams(vmem_limit_bytes=16 * 1024 * 1024),
        cost_estimate=pl.CostEstimate(
            flops=2 * got.size * select.shape[2], bytes_accessed=4 * got.size, transcendentals=0
        ),
    )(got, select)


def on_device(
    projection_gradient,
    acts,
    routes,
    gates,
    tenants,
    levels,
    scales,
    adapter_first_factors,
    adapter_second_factors,
):
    experts = lax.axis_size("expert")
    ring = lax.axis_size("y")
    half = lax.axis_index("xh")
    planes, hid, topk, toks = projection_gradient.shape
    width_rows = acts.shape[0]
    rank = adapter_first_factors.shape[3] // TENANT_COUNT
    cols = TENANT_COUNT * rank
    capacity = 5 * toks * topk // (4 * experts)
    room = -(-capacity // 16) * 16
    slots = experts * room
    own = planes * hid

    side = 64
    send_z, select_tok = route_call(
        routes.T,
        gates.T,
        tenants.reshape(1, toks),
        projection_gradient.reshape(own, topk * toks),
        experts, room, side
    )
    send_z = send_z.reshape(experts, room, own + side)
    send_z, levels, scales, acts = lax.optimization_barrier((send_z, levels, scales, acts))
    got_z = lax.all_to_all(send_z, "expert", 0, 0, tiled=True).reshape(slots, -1)

    adapter_first = adapter_first_factors[0]
    adapter_second = adapter_second_factors[0].reshape(own, cols)
    swap = [(0, 1), (1, 0)]
    kept_w, send_w = weight_call(half.reshape(1), levels[0], scales[0], adapter_first)
    send_x = dot(select_tok, acts, ((1,), (1,))).astype(BF).reshape(experts, room, width_rows)
    got_w = lax.ppermute(send_w, "xh", swap)
    got_z, send_x, kept_w = lax.optimization_barrier((got_z, send_x, kept_w))

    across_z = got_z.T
    own_z = across_z[:own]
    payload = jnp.concatenate([own_z, adapter_second], axis=1)
    gathered = lax.all_gather(payload.reshape(planes, hid, slots + cols), "y", axis=0, tiled=False)

    got_x = lax.all_to_all(send_x, "expert", 0, 0, tiled=True).reshape(slots, width_rows)
    gate_row = across_z[own].astype(F32)
    tenant_row = across_z[own + 1].astype(F32)
    one = tenant_row[None, :] == jnp.arange(TENANT_COUNT, dtype=F32)[:, None]
    down = lax.dot_general(
        adapter_first, got_x, (((1,), (1,)), ((), ())), preferred_element_type=F32
    ).reshape(planes, TENANT_COUNT, rank, slots)
    down = jnp.sum(jnp.where(one[None, :, None, :], down, 0.0), axis=1).reshape(
        planes * rank, slots
    )
    down = down + lax.ppermute(down, "xh", swap)
    down, got_w = lax.optimization_barrier((down, got_w))
    downs = lax.all_gather(down, "y", axis=0, tiled=False)

    pair_dx, back = pair_call(
        half.reshape(1), gathered, got_z, across_z, kept_w, got_w, adapter_first,
        rank, own, slots, experts
    )
    returned = lax.all_to_all(
        pair_dx.reshape((2 * experts,) + pair_dx.shape[2:]), ("xh", "expert"), 0, 0, tiled=True
    ).reshape(pair_dx.shape)
    ranks = jnp.concatenate(
        [jnp.sum(downs, axis=0), back + lax.ppermute(back, "xh", swap)], axis=0
    )
    scaled = (ranks * (ADAPTER_SCALE * gate_row)[None, :]).astype(BF)
    spread = jnp.where(
        one[None, :, None, :], scaled.reshape(2 * planes, 1, rank, slots), jnp.zeros((), BF)
    ).reshape(2, planes, cols, slots)
    second_grad = jnp.stack(
        [
            dot(own_z[j * hid : (j + 1) * hid], spread[0, j], ((1,), (1,)))
            for j in range(planes)
        ]
    )
    first_grad = jnp.stack([dot(got_x, spread[1, j].T, ((0,), (0,))) for j in range(planes)])
    returned, first_grad, second_grad = lax.optimization_barrier((returned, first_grad, second_grad))
    input_grad = combine_call(returned, select_tok.reshape(experts, room, toks), width_rows)
    return input_grad, first_grad[None], second_grad[None]


def solution(mesh):
    groups, experts = mesh.devices.shape
    split = Mesh(mesh.devices.reshape(2, groups // 2, experts), ("xh", "y", "expert"))
    dp = ("xh", "y")
    factors = P("expert", None, dp, None)
    return jax.shard_map(
        on_device,
        mesh=split,
        in_specs=(
            P(None, dp, None, "expert"),
            P(dp, "expert"),
            P("expert", None),
            P("expert", None),
            P("expert"),
            factors,
            factors,
            factors,
            factors,
        ),
        out_specs=(P(dp, "expert"), factors, factors),
        check_vma=False,
    )
```

```python
import functools

import jax
import jax.numpy as jnp
from jax import lax
from jax.experimental import pallas as pl
from jax.experimental.pallas import tpu as pltpu
from jax.sharding import Mesh
from jax.sharding import PartitionSpec as P

TENANT_COUNT = 8
GROUP = 64
ADAPTER_SCALE = 2.0
BF = jnp.bfloat16
F32 = jnp.float32


def dot(a, b, dims):
    return lax.dot_general(a, b, (dims, ((), ())), preferred_element_type=F32)


def route_kernel(room, side, route_ref, gate_ref, tenant_ref, grad_ref, send_ref, select_ref, full_ref):
    topk, toks = route_ref.shape
    own, slots = grad_ref.shape[0], send_ref.shape[0]
    expert_ids = lax.broadcasted_iota(jnp.int32, (slots // room, toks), 0)
    named = [route_ref[k : k + 1, :] == expert_ids for k in range(topk)]
    member = sum(jnp.where(m, 1.0, 0.0) for m in named).astype(BF)
    row = lax.broadcasted_iota(jnp.int32, (toks, toks), 0)
    before = jnp.where(row < lax.broadcasted_iota(jnp.int32, (toks, toks), 1), 1.0, 0.0).astype(BF)
    place = dot(member, before, ((1,), (0,))).astype(jnp.int32) + expert_ids * room
    slot_ids = lax.broadcasted_iota(jnp.int32, (slots, toks), 0)
    line = lax.broadcasted_iota(jnp.int32, (side, toks), 0)
    tenant = tenant_ref[...].astype(F32)
    total, either = 0.0, 0.0
    for k in range(topk):
        position = jnp.sum(jnp.where(named[k], place, 0), axis=0, keepdims=True)
        chosen = jnp.where(slot_ids == position, 1.0, 0.0)
        either = either + chosen
        gate = gate_ref[k : k + 1, :].astype(F32)
        extra = jnp.where(line == 0, gate, jnp.where(line == 1, tenant, 0.0))
        full_ref[:own, :] = grad_ref[:, k * toks : (k + 1) * toks]
        full_ref[own:, :] = extra.astype(BF)
        total = total + dot(chosen.astype(BF), full_ref[...], ((1,), (1,)))
    send_ref[...] = total.astype(BF)
    select_ref[...] = either.astype(BF)


def route_call(routes, gates, tenants, grads, experts, room, side):
    toks, own, slots = tenants.shape[1], grads.shape[0], experts * room
    vmem = pl.BlockSpec(memory_space=pltpu.VMEM)
    return pl.pallas_call(
        functools.partial(route_kernel, room, side),
        in_specs=[vmem] * 4,
        out_specs=[vmem, vmem],
        out_shape=[
            jax.ShapeDtypeStruct((slots, own + side), BF),
            jax.ShapeDtypeStruct((slots, toks), BF),
        ],
        scratch_shapes=[pltpu.VMEM((own + side, toks), BF)],
        compiler_params=pltpu.CompilerParams(vmem_limit_bytes=16 * 1024 * 1024),
        cost_estimate=pl.CostEstimate(
            flops=4 * slots * toks * (own + side), bytes_accessed=4 * slots * toks, transcendentals=0
        ),
    )(routes, gates, tenants, grads)


def weight_kernel(group, half_ref, level_ref, scale_ref, first_ref, kept_ref, sent_ref):
    planes, rows, width = level_ref.shape
    mid = width // 2
    near = pl.multiple_of(half_ref[0] * mid, 128)
    far = pl.multiple_of((1 - half_ref[0]) * mid, 128)

    def rounded(j, start):
        parts = []
        for g in range(rows // group):
            level = level_ref[j, g * group : (g + 1) * group, pl.ds(start, mid)].astype(F32)
            scale = scale_ref[j, g : g + 1, pl.ds(start, mid)].astype(F32)
            parts.append((level * scale).astype(BF))
        return jnp.concatenate(parts, axis=0)

    for j in range(planes):
        sent_ref[j, :, :mid] = rounded(j, far)
        sent_ref[j, :, mid:] = first_ref[j]
        kept_ref[j] = rounded(j, near).T


def weight_call(half, levels, scales, first):
    planes, rows, width = levels.shape
    mid, cols = width // 2, first.shape[2]
    vmem = pl.BlockSpec(memory_space=pltpu.VMEM)
    return pl.pallas_call(
        functools.partial(weight_kernel, GROUP),
        in_specs=[pl.BlockSpec(memory_space=pltpu.SMEM), vmem, vmem, vmem],
        out_specs=[vmem, vmem],
        out_shape=[
            jax.ShapeDtypeStruct((planes, mid, rows), BF),
            jax.ShapeDtypeStruct((planes, rows, mid + cols), BF),
        ],
        compiler_params=pltpu.CompilerParams(vmem_limit_bytes=16 * 1024 * 1024),
        cost_estimate=pl.CostEstimate(
            flops=planes * rows * width, bytes_accessed=4 * planes * rows * width, transcendentals=0
        ),
    )(half, levels, scales, first)


def pair_kernel(
    rank, tile, own, half_ref, z_ref, rows_ref, cols_ref, kept_ref, got_ref, first_ref,
    dx_ref, back_ref, turned_ref
):
    ring, planes, hid, wide = z_ref.shape
    room, depth, width = dx_ref.shape[2] * 128 // kept_ref.shape[2], kept_ref.shape[1], kept_ref.shape[2]
    slots = dx_ref.shape[1] * room
    tiles, cols = slots // tile, wide - slots
    some, full = tile // room, width // 128
    for j in range(planes):
        turned_ref[j] = got_ref[j, :, :depth].T
    at = own
    half = half_ref[0]
    lane = lax.broadcasted_iota(jnp.int32, (tile, cols), 1)

    def step(i):
        place = pl.ds(i * tile, tile)
        gate = rows_ref[place, at : at + 1].astype(F32)
        tenant = rows_ref[place, at + 1 : at + 2].astype(F32)
        tenant_row = cols_ref[own + 1 : own + 2, place].astype(F32)
        mine = (lane // rank).astype(F32) == tenant
        z, scaled = [], []
        for j in range(planes):
            z.append(z_ref[:, j, :, place].reshape(ring * hid, tile).T)
            second = z_ref[:, j, :, slots:].reshape(ring * hid, cols)
            back = dot(z[j], second, ((1,), (0,)))
            scaled.append(jnp.where(mine, back * (ADAPTER_SCALE * gate), 0.0).astype(BF))
            across = back.T
            total = jnp.zeros((rank, tile), F32)
            for t in range(cols // rank):
                part = across[t * rank : (t + 1) * rank]
                total += jnp.where(tenant_row == float(t), part, 0.0)
            back_ref[j * rank : (j + 1) * rank, place] = total
        firsts = [first_ref[j] for j in range(planes)], [got_ref[j, :, depth:] for j in range(planes)]
        both = ((half, kept_ref, firsts[0]), (1 - half, turned_ref, firsts[1]))
        from_experts = pl.ds(i * some, some)
        for where, weight, first in both:
            frozen = sum(dot(z[j], weight[j], ((1,), (0,))) for j in range(planes))
            extra = sum(dot(scaled[j], first[j], ((1,), (1,))) for j in range(planes))
            dx = (gate * frozen + extra).astype(BF).reshape(some, room, width)
            for c in range(full):
                dx_ref[where, from_experts, c * room : (c + 1) * room, :] = dx[:, :, c * 128 : (c + 1) * 128]
            rest = dx[:, :, full * 128 :]
            rest = jnp.concatenate([rest[:, : room // 2], rest[:, room // 2 :]], axis=2)
            dx_ref[where, from_experts, full * room :, :] = rest

    for i in range(tiles):
        step(i)


def pair_call(half, gathered, got_z, across_z, kept, got, first, rank, own, slots, experts):
    ring, planes, hid, wide = gathered.shape
    cols = wide - slots
    depth, width = kept.shape[1:]
    tile = 512 if slots % 512 == 0 else slots
    vmem = pl.BlockSpec(memory_space=pltpu.VMEM)
    return pl.pallas_call(
        functools.partial(pair_kernel, rank, tile, own),
        in_specs=[
            pl.BlockSpec(memory_space=pltpu.SMEM),
            vmem,
            vmem,
            vmem,
            vmem,
            vmem,
            vmem,
        ],
        out_specs=[vmem, vmem],
        out_shape=[
            jax.ShapeDtypeStruct((2, experts, slots // experts * width // 128, 128), BF),
            jax.ShapeDtypeStruct((planes * rank, slots), F32),
        ],
        scratch_shapes=[pltpu.VMEM((planes, depth, width), BF)],
        compiler_params=pltpu.CompilerParams(vmem_limit_bytes=48 * 1024 * 1024),
        cost_estimate=pl.CostEstimate(
            flops=2 * slots * planes * depth * (2 * width + 2 * cols),
            bytes_accessed=2 * planes * depth * (wide + 2 * width) + 4 * slots * width,
            transcendentals=0,
        ),
    )(half, gathered, got_z, across_z, kept, got, first)


def combine_kernel(got_ref, select_ref, out_ref):
    halves, experts, _, lanes = got_ref.shape
    room, toks = select_ref.shape[1:]
    full = out_ref.shape[0] // lanes

    def total(start, size, chosen):
        parts = [got_ref[h, :, start : start + size, :] for h in range(halves)]
        parts = [p.reshape(experts * size, lanes) for p in parts]
        return sum(dot(p, chosen, ((0,), (0,))) for p in parts)

    select = select_ref[...].reshape(experts * room, toks)
    for c in range(full):
        out_ref[c * lanes : (c + 1) * lanes, :] = total(c * room, room, select).astype(BF)
    low = select_ref[:, : room // 2].reshape(experts * room // 2, toks)
    high = select_ref[:, room // 2 :].reshape(experts * room // 2, toks)
    first = total(full * room, room // 2, low)[: lanes // 2]
    second = total(full * room, room // 2, high)[lanes // 2 :]
    out_ref[full * lanes :, :] = (first + second).astype(BF)


def combine_call(got, select, width):
    vmem = pl.BlockSpec(memory_space=pltpu.VMEM)
    return pl.pallas_call(
        combine_kernel,
        in_specs=[vmem, vmem],
        out_specs=vmem,
        out_shape=jax.ShapeDtypeStruct((width, select.shape[2]), BF),
        compiler_params=pltpu.CompilerParams(vmem_limit_bytes=16 * 1024 * 1024),
        cost_estimate=pl.CostEstimate(
            flops=2 * got.size * select.shape[2], bytes_accessed=4 * got.size, transcendentals=0
        ),
    )(got, select)


def on_device(
    projection_gradient,
    acts,
    routes,
    gates,
    tenants,
    levels,
    scales,
    adapter_first_factors,
    adapter_second_factors,
):
    experts = lax.axis_size("expert")
    ring = lax.axis_size("y")
    half = lax.axis_index("xh")
    planes, hid, topk, toks = projection_gradient.shape
    width_rows = acts.shape[0]
    rank = adapter_first_factors.shape[3] // TENANT_COUNT
    cols = TENANT_COUNT * rank
    capacity = 5 * toks * topk // (4 * experts)
    room = -(-capacity // 16) * 16
    slots = experts * room
    own = planes * hid

    side = 64
    send_z, select_tok = route_call(
        routes.T,
        gates.T,
        tenants.reshape(1, toks),
        projection_gradient.reshape(own, topk * toks),
        experts, room, side
    )
    send_z = send_z.reshape(experts, room, own + side)
    send_z, levels, scales, acts = lax.optimization_barrier((send_z, levels, scales, acts))
    got_z = lax.all_to_all(send_z, "expert", 0, 0, tiled=True).reshape(slots, -1)

    adapter_first = adapter_first_factors[0]
    adapter_second = adapter_second_factors[0].reshape(own, cols)
    swap = [(0, 1), (1, 0)]
    kept_w, send_w = weight_call(half.reshape(1), levels[0], scales[0], adapter_first)
    send_x = dot(select_tok, acts, ((1,), (1,))).astype(BF).reshape(experts, room, width_rows)
    got_w = lax.ppermute(send_w, "xh", swap)
    got_z, send_x, kept_w = lax.optimization_barrier((got_z, send_x, kept_w))

    across_z = got_z.T
    own_z = across_z[:own]
    payload = jnp.concatenate([own_z, adapter_second], axis=1)
    gathered = lax.all_gather(payload.reshape(planes, hid, slots + cols), "y", axis=0, tiled=False)

    got_x = lax.all_to_all(send_x, "expert", 0, 0, tiled=True).reshape(slots, width_rows)
    gate_row = across_z[own].astype(F32)
    tenant_row = across_z[own + 1].astype(F32)
    one = tenant_row[None, :] == jnp.arange(TENANT_COUNT, dtype=F32)[:, None]
    down = lax.dot_general(
        adapter_first, got_x, (((1,), (1,)), ((), ())), preferred_element_type=F32
    ).reshape(planes, TENANT_COUNT, rank, slots)
    down = jnp.sum(jnp.where(one[None, :, None, :], down, 0.0), axis=1).reshape(
        planes * rank, slots
    )
    down = down + lax.ppermute(down, "xh", swap)
    down, got_w = lax.optimization_barrier((down, got_w))
    downs = lax.all_gather(down, "y", axis=0, tiled=False)

    pair_dx, back = pair_call(
        half.reshape(1), gathered, got_z, across_z, kept_w, got_w, adapter_first,
        rank, own, slots, experts
    )
    returned = lax.all_to_all(
        pair_dx.reshape((2 * experts,) + pair_dx.shape[2:]), ("xh", "expert"), 0, 0, tiled=True
    ).reshape(pair_dx.shape)
    ranks = jnp.concatenate(
        [jnp.sum(downs, axis=0), back + lax.ppermute(back, "xh", swap)], axis=0
    )
    scaled = (ranks * (ADAPTER_SCALE * gate_row)[None, :]).astype(BF)
    spread = jnp.where(
        one[None, :, None, :], scaled.reshape(2 * planes, 1, rank, slots), jnp.zeros((), BF)
    ).reshape(2, planes, cols, slots)
    second_grad = jnp.stack(
        [
            dot(own_z[j * hid : (j + 1) * hid], spread[0, j], ((1,), (1,)))
            for j in range(planes)
        ]
    )
    first_grad = jnp.stack([dot(got_x, spread[1, j].T, ((0,), (0,))) for j in range(planes)])
    returned, first_grad, second_grad = lax.optimization_barrier((returned, first_grad, second_grad))
    input_grad = combine_call(returned, select_tok.reshape(experts, room, toks), width_rows)
    return input_grad, first_grad[None], second_grad[None]


def solution(mesh):
    groups, experts = mesh.devices.shape
    split = Mesh(mesh.devices.reshape(2, groups // 2, experts), ("xh", "y", "expert"))
    dp = ("xh", "y")
    factors = P("expert", None, dp, None)
    return jax.shard_map(
        on_device,
        mesh=split,
        in_specs=(
            P(None, dp, None, "expert"),
            P(dp, "expert"),
            P("expert", None),
            P("expert", None),
            P("expert"),
            factors,
            factors,
            factors,
            factors,
        ),
        out_specs=(P(dp, "expert"), factors, factors),
        check_vma=False,
    )
```

```python
import functools

import jax
import jax.numpy as jnp
from jax import lax
from jax.experimental import pallas as pl
from jax.experimental.pallas import tpu as pltpu
from jax.sharding import Mesh
from jax.sharding import PartitionSpec as P

TENANT_COUNT = 8
GROUP = 64
ADAPTER_SCALE = 2.0
BF = jnp.bfloat16
F32 = jnp.float32


def dot(a, b, dims):
    return lax.dot_general(a, b, (dims, ((), ())), preferred_element_type=F32)


def route_kernel(room, side, route_ref, gate_ref, tenant_ref, grad_ref, send_ref, select_ref, full_ref):
    topk, toks = route_ref.shape
    own, slots = grad_ref.shape[0], send_ref.shape[0]
    expert_ids = lax.broadcasted_iota(jnp.int32, (slots // room, toks), 0)
    named = [route_ref[k : k + 1, :] == expert_ids for k in range(topk)]
    member = sum(jnp.where(m, 1.0, 0.0) for m in named).astype(BF)
    row = lax.broadcasted_iota(jnp.int32, (toks, toks), 0)
    before = jnp.where(row < lax.broadcasted_iota(jnp.int32, (toks, toks), 1), 1.0, 0.0).astype(BF)
    place = dot(member, before, ((1,), (0,))).astype(jnp.int32) + expert_ids * room
    slot_ids = lax.broadcasted_iota(jnp.int32, (slots, toks), 0)
    line = lax.broadcasted_iota(jnp.int32, (side, toks), 0)
    tenant = tenant_ref[...].astype(F32)
    total, either = 0.0, 0.0
    for k in range(topk):
        position = jnp.sum(jnp.where(named[k], place, 0), axis=0, keepdims=True)
        chosen = jnp.where(slot_ids == position, 1.0, 0.0)
        either = either + chosen
        gate = gate_ref[k : k + 1, :].astype(F32)
        extra = jnp.where(line == 0, gate, jnp.where(line == 1, tenant, 0.0))
        full_ref[:own, :] = grad_ref[:, k * toks : (k + 1) * toks]
        full_ref[own:, :] = extra.astype(BF)
        total = total + dot(chosen.astype(BF), full_ref[...], ((1,), (1,)))
    send_ref[...] = total.astype(BF)
    select_ref[...] = either.astype(BF)


def route_call(routes, gates, tenants, grads, experts, room, side):
    toks, own, slots = tenants.shape[1], grads.shape[0], experts * room
    vmem = pl.BlockSpec(memory_space=pltpu.VMEM)
    return pl.pallas_call(
        functools.partial(route_kernel, room, side),
        in_specs=[vmem] * 4,
        out_specs=[vmem, vmem],
        out_shape=[
            jax.ShapeDtypeStruct((slots, own + side), BF),
            jax.ShapeDtypeStruct((slots, toks), BF),
        ],
        scratch_shapes=[pltpu.VMEM((own + side, toks), BF)],
        compiler_params=pltpu.CompilerParams(vmem_limit_bytes=16 * 1024 * 1024),
        cost_estimate=pl.CostEstimate(
            flops=4 * slots * toks * (own + side), bytes_accessed=4 * slots * toks, transcendentals=0
        ),
    )(routes, gates, tenants, grads)


def weight_kernel(group, half_ref, level_ref, scale_ref, first_ref, kept_ref, sent_ref):
    planes, rows, width = level_ref.shape
    mid = width // 2
    near = pl.multiple_of(half_ref[0] * mid, 128)
    far = pl.multiple_of((1 - half_ref[0]) * mid, 128)

    def rounded(j, start):
        parts = []
        for g in range(rows // group):
            level = level_ref[j, g * group : (g + 1) * group, pl.ds(start, mid)].astype(F32)
            scale = scale_ref[j, g : g + 1, pl.ds(start, mid)].astype(F32)
            parts.append((level * scale).astype(BF))
        return jnp.concatenate(parts, axis=0)

    for j in range(planes):
        sent_ref[j, :, :mid] = rounded(j, far)
        sent_ref[j, :, mid:] = first_ref[j]
        kept_ref[j] = rounded(j, near).T


def weight_call(half, levels, scales, first):
    planes, rows, width = levels.shape
    mid, cols = width // 2, first.shape[2]
    vmem = pl.BlockSpec(memory_space=pltpu.VMEM)
    return pl.pallas_call(
        functools.partial(weight_kernel, GROUP),
        in_specs=[pl.BlockSpec(memory_space=pltpu.SMEM), vmem, vmem, vmem],
        out_specs=[vmem, vmem],
        out_shape=[
            jax.ShapeDtypeStruct((planes, mid, rows), BF),
            jax.ShapeDtypeStruct((planes, rows, mid + cols), BF),
        ],
        compiler_params=pltpu.CompilerParams(vmem_limit_bytes=16 * 1024 * 1024),
        cost_estimate=pl.CostEstimate(
            flops=planes * rows * width, bytes_accessed=4 * planes * rows * width, transcendentals=0
        ),
    )(half, levels, scales, first)


def pair_kernel(
    rank, tile, own, half_ref, z_ref, rows_ref, cols_ref, kept_ref, got_ref, first_ref,
    dx_ref, back_ref, turned_ref
):
    ring, planes, hid, wide = z_ref.shape
    room, depth, width = dx_ref.shape[2] * 128 // kept_ref.shape[2], kept_ref.shape[1], kept_ref.shape[2]
    slots = dx_ref.shape[1] * room
    tiles, cols = slots // tile, wide - slots
    some, full = tile // room, width // 128
    for j in range(planes):
        turned_ref[j] = got_ref[j, :, :depth].T
    at = own
    half = half_ref[0]
    lane = lax.broadcasted_iota(jnp.int32, (tile, cols), 1)

    def step(i):
        place = pl.ds(i * tile, tile)
        gate = rows_ref[place, at : at + 1].astype(F32)
        tenant = rows_ref[place, at + 1 : at + 2].astype(F32)
        tenant_row = cols_ref[own + 1 : own + 2, place].astype(F32)
        mine = (lane // rank).astype(F32) == tenant
        z, scaled = [], []
        for j in range(planes):
            z.append(z_ref[:, j, :, place].reshape(ring * hid, tile).T)
            second = z_ref[:, j, :, slots:].reshape(ring * hid, cols)
            back = dot(z[j], second, ((1,), (0,)))
            scaled.append(jnp.where(mine, back * (ADAPTER_SCALE * gate), 0.0).astype(BF))
            across = back.T
            total = jnp.zeros((rank, tile), F32)
            for t in range(cols // rank):
                part = across[t * rank : (t + 1) * rank]
                total += jnp.where(tenant_row == float(t), part, 0.0)
            back_ref[j * rank : (j + 1) * rank, place] = total
        firsts = [first_ref[j] for j in range(planes)], [got_ref[j, :, depth:] for j in range(planes)]
        both = ((half, kept_ref, firsts[0]), (1 - half, turned_ref, firsts[1]))
        from_experts = pl.ds(i * some, some)
        for where, weight, first in both:
            frozen = sum(dot(z[j], weight[j], ((1,), (0,))) for j in range(planes))
            extra = sum(dot(scaled[j], first[j], ((1,), (1,))) for j in range(planes))
            dx = (gate * frozen + extra).astype(BF).reshape(some, room, width)
            for c in range(full):
                dx_ref[where, from_experts, c * room : (c + 1) * room, :] = dx[:, :, c * 128 : (c + 1) * 128]
            rest = dx[:, :, full * 128 :]
            rest = jnp.concatenate([rest[:, : room // 2], rest[:, room // 2 :]], axis=2)
            dx_ref[where, from_experts, full * room :, :] = rest

    for i in range(tiles):
        step(i)


def pair_call(half, gathered, got_z, across_z, kept, got, first, rank, own, slots, experts):
    ring, planes, hid, wide = gathered.shape
    cols = wide - slots
    depth, width = kept.shape[1:]
    tile = slots
    vmem = pl.BlockSpec(memory_space=pltpu.VMEM)
    return pl.pallas_call(
        functools.partial(pair_kernel, rank, tile, own),
        in_specs=[
            pl.BlockSpec(memory_space=pltpu.SMEM),
            vmem,
            vmem,
            vmem,
            vmem,
            vmem,
            vmem,
        ],
        out_specs=[vmem, vmem],
        out_shape=[
            jax.ShapeDtypeStruct((2, experts, slots // experts * width // 128, 128), BF),
            jax.ShapeDtypeStruct((planes * rank, slots), F32),
        ],
        scratch_shapes=[pltpu.VMEM((planes, depth, width), BF)],
        compiler_params=pltpu.CompilerParams(vmem_limit_bytes=48 * 1024 * 1024),
        cost_estimate=pl.CostEstimate(
            flops=2 * slots * planes * depth * (2 * width + 2 * cols),
            bytes_accessed=2 * planes * depth * (wide + 2 * width) + 4 * slots * width,
            transcendentals=0,
        ),
    )(half, gathered, got_z, across_z, kept, got, first)


def combine_kernel(got_ref, select_ref, out_ref):
    halves, experts, _, lanes = got_ref.shape
    room, toks = select_ref.shape[1:]
    full = out_ref.shape[0] // lanes

    def total(start, size, chosen):
        parts = [got_ref[h, :, start : start + size, :] for h in range(halves)]
        parts = [p.reshape(experts * size, lanes) for p in parts]
        return sum(dot(p, chosen, ((0,), (0,))) for p in parts)

    select = select_ref[...].reshape(experts * room, toks)
    for c in range(full):
        out_ref[c * lanes : (c + 1) * lanes, :] = total(c * room, room, select).astype(BF)
    low = select_ref[:, : room // 2].reshape(experts * room // 2, toks)
    high = select_ref[:, room // 2 :].reshape(experts * room // 2, toks)
    first = total(full * room, room // 2, low)[: lanes // 2]
    second = total(full * room, room // 2, high)[lanes // 2 :]
    out_ref[full * lanes :, :] = (first + second).astype(BF)


def combine_call(got, select, width):
    vmem = pl.BlockSpec(memory_space=pltpu.VMEM)
    return pl.pallas_call(
        combine_kernel,
        in_specs=[vmem, vmem],
        out_specs=vmem,
        out_shape=jax.ShapeDtypeStruct((width, select.shape[2]), BF),
        compiler_params=pltpu.CompilerParams(vmem_limit_bytes=16 * 1024 * 1024),
        cost_estimate=pl.CostEstimate(
            flops=2 * got.size * select.shape[2], bytes_accessed=4 * got.size, transcendentals=0
        ),
    )(got, select)


def on_device(
    projection_gradient,
    acts,
    routes,
    gates,
    tenants,
    levels,
    scales,
    adapter_first_factors,
    adapter_second_factors,
):
    experts = lax.axis_size("expert")
    ring = lax.axis_size("y")
    half = lax.axis_index("xh")
    planes, hid, topk, toks = projection_gradient.shape
    width_rows = acts.shape[0]
    rank = adapter_first_factors.shape[3] // TENANT_COUNT
    cols = TENANT_COUNT * rank
    capacity = 5 * toks * topk // (4 * experts)
    room = -(-capacity // 16) * 16
    slots = experts * room
    own = planes * hid

    side = 64
    send_z, select_tok = route_call(
        routes.T,
        gates.T,
        tenants.reshape(1, toks),
        projection_gradient.reshape(own, topk * toks),
        experts, room, side
    )
    send_z = send_z.reshape(experts, room, own + side)
    send_z, levels, scales, acts = lax.optimization_barrier((send_z, levels, scales, acts))
    got_z = lax.all_to_all(send_z, "expert", 0, 0, tiled=True).reshape(slots, -1)

    adapter_first = adapter_first_factors[0]
    adapter_second = adapter_second_factors[0].reshape(own, cols)
    swap = [(0, 1), (1, 0)]
    kept_w, send_w = weight_call(half.reshape(1), levels[0], scales[0], adapter_first)
    send_x = dot(select_tok, acts, ((1,), (1,))).astype(BF).reshape(experts, room, width_rows)
    got_w = lax.ppermute(send_w, "xh", swap)
    got_z, send_x, kept_w = lax.optimization_barrier((got_z, send_x, kept_w))

    across_z = got_z.T
    own_z = across_z[:own]
    payload = jnp.concatenate([own_z, adapter_second], axis=1)
    gathered = lax.all_gather(payload.reshape(planes, hid, slots + cols), "y", axis=0, tiled=False)

    got_x = lax.all_to_all(send_x, "expert", 0, 0, tiled=True).reshape(slots, width_rows)
    gate_row = across_z[own].astype(F32)
    tenant_row = across_z[own + 1].astype(F32)
    one = tenant_row[None, :] == jnp.arange(TENANT_COUNT, dtype=F32)[:, None]
    down = lax.dot_general(
        adapter_first, got_x, (((1,), (1,)), ((), ())), preferred_element_type=F32
    ).reshape(planes, TENANT_COUNT, rank, slots)
    down = jnp.sum(jnp.where(one[None, :, None, :], down, 0.0), axis=1).reshape(
        planes * rank, slots
    )
    down = down + lax.ppermute(down, "xh", swap)
    down, got_w = lax.optimization_barrier((down, got_w))
    downs = lax.all_gather(down, "y", axis=0, tiled=False)

    pair_dx, back = pair_call(
        half.reshape(1), gathered, got_z, across_z, kept_w, got_w, adapter_first,
        rank, own, slots, experts
    )
    returned = lax.all_to_all(
        pair_dx.reshape((2 * experts,) + pair_dx.shape[2:]), ("xh", "expert"), 0, 0, tiled=True
    ).reshape(pair_dx.shape)
    ranks = jnp.concatenate(
        [jnp.sum(downs, axis=0), back + lax.ppermute(back, "xh", swap)], axis=0
    )
    scaled = (ranks * (ADAPTER_SCALE * gate_row)[None, :]).astype(BF)
    spread = jnp.where(
        one[None, :, None, :], scaled.reshape(2 * planes, 1, rank, slots), jnp.zeros((), BF)
    ).reshape(2, planes, cols, slots)
    second_grad = jnp.stack(
        [
            dot(own_z[j * hid : (j + 1) * hid], spread[0, j], ((1,), (1,)))
            for j in range(planes)
        ]
    )
    first_grad = jnp.stack([dot(got_x, spread[1, j].T, ((0,), (0,))) for j in range(planes)])
    returned, first_grad, second_grad = lax.optimization_barrier((returned, first_grad, second_grad))
    input_grad = combine_call(returned, select_tok.reshape(experts, room, toks), width_rows)
    return input_grad, first_grad[None], second_grad[None]


def solution(mesh):
    groups, experts = mesh.devices.shape
    split = Mesh(mesh.devices.reshape(2, groups // 2, experts), ("xh", "y", "expert"))
    dp = ("xh", "y")
    factors = P("expert", None, dp, None)
    return jax.shard_map(
        on_device,
        mesh=split,
        in_specs=(
            P(None, dp, None, "expert"),
            P(dp, "expert"),
            P("expert", None),
            P("expert", None),
            P("expert"),
            factors,
            factors,
            factors,
            factors,
        ),
        out_specs=(P(dp, "expert"), factors, factors),
        check_vma=False,
    )
```
